256 devices in a mesh: seq: 8 (over x, core), exp: 32 (over y, z).
Axes of the slice: x: 4, y: 4, z: 8, core: 2. Of those that a mesh axis runs over, the one named last changes fastest.
Arguments:
- heads_primal: bfloat16 [32768, 1280], P('exp', 'seq'), may hold values from -6 to 6
- heads_tangent: bfloat16 [32768, 1280], P('exp', 'seq'), may hold values from -6 to 6
- expert_ids: int32 [32768, 2], P(('exp', 'seq')), may hold values from 0 to 15, all different within a row; in each aligned block of 128 rows (0 to 127, 128 to 255, ...) at most 18 rows name the same one
- gate_weights: float32 [32768, 2], P(('exp', 'seq')), may hold values from 0.2 to 1
- gate_tangent: float32 [32768, 2], P(('exp', 'seq')), may hold values from -1 to 1
- w_gate: bfloat16 [32, 1280, 1536], P('exp'), may hold values from -0.15625 to 0.15625
- w_up: bfloat16 [32, 1280, 1536], P('exp'), may hold values from -0.15625 to 0.15625
- w_down: bfloat16 [32, 1536, 1280], P('exp'), may hold values from -0.109375 to 0.109375
Outputs:
- moe_out: bfloat16 [32768, 1280], P(('exp', 'seq'))
- moe_tangent: bfloat16 [32768, 1280], P(('exp', 'seq'))
The draws below stay inside these ranges and needn't reach their ends.
Inputs may be any that keep to these rules, and one draw needn't show every extreme that they name: `expert_ids`: each token names two different experts; in the rows of one device (aligned blocks of 128 tokens) no expert is named more than 18 times.
All inputs are finite; a program needn't handle non-finite values.
Results may differ from the reference program's by a relative error of at most 0.0065.
Values may be sent and summed in bfloat16 or wider, within the bound.
A program may use at most 64 MiB of HBM per device.

```python
import math
import jax
import jax.numpy as jnp
import numpy as np
from jax import lax

FF = 3072
TOK_DEV = 128
FEAT = 1280
FF_HALF = 1536
EXPERTS = 16
CAP = 18
TOKENS = 32768
N_EXP = 32


def levels(key, shape, split, smallest, largest):
    level = 1.0
    for dim, blocks in split:
        draws = jax.random.uniform(jax.random.fold_in(jax.random.fold_in(key, 6), dim), (blocks,), jnp.float32, smallest / len(split), largest / len(split))
        level = level * jnp.repeat(jnp.exp(draws), shape[dim] // blocks).reshape((-1,) + (1,) * (len(shape) - 1 - dim))
    return level


def assign_block(own_key, own, number, rows, amount, top, most, lean):
    sequence = jax.random.permutation(own_key, amount)
    crowded, ordinary = load_shares(amount, rows * top, most, lean, True), load_shares(amount, rows * top, most, lean, False)
    places = jnp.arange(amount)

    def named(tallies, offset_by):
        used = int((tallies > 0).sum())
        fixed = max(1, used // 4)
        shifted = fixed + (places - fixed + offset_by * (used - fixed)) % max(1, amount - fixed)
        return jnp.zeros((amount,), jnp.int32).at[sequence[jnp.where(places < fixed, places, shifted)]].set(jnp.asarray(tallies, jnp.int32))

    tallies = jnp.where(number % 4 == 0, named(crowded, number // 4), named(ordinary, number - number // 4 - 1))
    mixed = jax.random.permutation(jax.random.fold_in(own, 3), amount)
    donor, receiver = mixed[0:amount // 2 * 2:2], mixed[1:amount // 2 * 2:2]
    slack = jnp.minimum(tallies[donor] - 1, most - tallies[receiver]) // 2
    slack = jnp.where((donor == sequence[0]) | (receiver == sequence[0]) | (tallies[receiver] == 0), 0, jnp.maximum(slack, 0))
    shifted = jax.random.randint(jax.random.fold_in(own, 4), (amount // 2,), 0, 1 << 20) % (slack + 1)
    tallies = tallies.at[donor].add(-shifted).at[receiver].add(shifted)
    items = jnp.searchsorted(jnp.cumsum(tallies), jnp.arange(rows * top), side="right").astype(jnp.int32)
    listing = items.reshape(top, rows).T
    listing = listing[jax.random.permutation(jax.random.fold_in(own, 1), rows)]
    offset_by = jax.random.randint(jax.random.fold_in(own, 2), (rows, 1), 0, top)
    return jnp.take_along_axis(listing, (jnp.arange(top)[None, :] + offset_by) % top, axis=1)


def load_shares(amount, total, reach, skew, full):
    weights = [(1 << 20) // math.isqrt(grade ** skew) + 1 for grade in range(1, amount + 1)]
    largest = reach if full else min(reach, max(-(-total // amount), total * weights[0] // sum(weights)))
    least = 1 if total - largest >= amount - 1 else 0
    counts, spare = [largest] + [least] * (amount - 1), total - largest - least * (amount - 1)
    while spare > 0:
        movable = [i for i in range(1, amount) if counts[i] < largest] or [i for i in range(1, amount) if counts[i] < reach]
        pool, budget = sum([weights[i] for i in movable]), spare
        for i in movable:
            extra = min(reach - counts[i], max(1, budget * weights[i] // pool), spare)
            counts[i] = counts[i] + extra
            spare = spare - extra
    return np.array(counts)


def normal_values(stream_key, shape, scale, reach, split=(), held_as=jnp.bfloat16):
    values = scale * jax.random.normal(stream_key, shape, jnp.float32)
    if split:
        values = values * levels(stream_key, shape, split, -0.22, 0.18)
    return jnp.clip(values, -reach, reach).astype(held_as)


def setup_inputs(seed: int = 0) -> dict:
    seeds = jax.random.split(jax.random.key(seed), 9)
    heads_primal = normal_values(seeds[0], (TOKENS, FEAT), 1.0, 6.0, ((0, 32), (1, 8)))
    heads_tangent = normal_values(seeds[1], (TOKENS, FEAT), 1.0, 6.0, ((0, 32), (1, 8)))
    expert_ids_keys = jax.random.split(jax.random.fold_in(seeds[2], 1), TOKENS // TOK_DEV)
    expert_ids_turns = jax.random.permutation(jax.random.fold_in(seeds[2], 3), TOKENS // TOK_DEV)
    expert_ids = jax.vmap(lambda own, number: assign_block(jax.random.fold_in(seeds[2], 2), own, number, TOK_DEV, EXPERTS, 2, CAP, 2))(expert_ids_keys, expert_ids_turns).reshape((TOKENS, 2))
    gate_weights = jnp.clip(0.2 + 0.8 * jax.random.uniform(seeds[3], (TOKENS, 2), jnp.float32) ** levels(seeds[3], (TOKENS, 2), ((0, 256),), -0.2, 0.2), 0.2, 1.0)
    gate_tangent = jnp.clip(jax.random.uniform(seeds[4], (TOKENS, 2), jnp.float32, -1.0, 1.0) * levels(seeds[4], (TOKENS, 2), ((0, 256),), -0.4, 0.0), -1.0, 1.0)
    w_gate = normal_values(seeds[5], (N_EXP, FEAT, FF_HALF), FEAT ** -0.5, 0.15625, ((0, 32),))
    w_up = normal_values(seeds[6], (N_EXP, FEAT, FF_HALF), FEAT ** -0.5, 0.15625, ((0, 32),))
    w_down = normal_values(seeds[7], (N_EXP, FF_HALF, FEAT), FF ** -0.5, 0.109375, ((0, 32),))
    return dict(heads_primal=heads_primal, heads_tangent=heads_tangent, expert_ids=expert_ids, gate_weights=gate_weights, gate_tangent=gate_tangent, w_gate=w_gate, w_up=w_up, w_down=w_down)


def expert_half(rows, tans, gate_w, up_w, down_w):
    width = rows.shape[-1]
    lead = rows.shape[:-1]
    both = jnp.concatenate([rows.reshape(-1, width), tans.reshape(-1, width)], 0)
    count = both.shape[0] // 2
    gate_all = jnp.dot(both, gate_w, preferred_element_type=jnp.float32)
    up_all = jnp.dot(both, up_w, preferred_element_type=jnp.float32)
    pre_gate = gate_all[:count]
    tan_gate = gate_all[count:]
    pre_up = up_all[:count]
    tan_up = up_all[count:]
    sigma = jax.nn.sigmoid(pre_gate)
    swish = pre_gate * sigma
    hidden = (swish * pre_up).astype(jnp.bfloat16)
    slope = sigma * (1.0 + pre_gate * (1.0 - sigma))
    hidden_tan = (slope * tan_gate * pre_up + swish * tan_up).astype(jnp.bfloat16)
    parts = jnp.dot(jnp.concatenate([hidden, hidden_tan], 0), down_w, preferred_element_type=jnp.float32).astype(jnp.bfloat16)
    return parts[:count].reshape(lead + (width,)), parts[count:].reshape(lead + (width,))


def reference(heads_primal, heads_tangent, expert_ids, gate_weights, gate_tangent, w_gate, w_up, w_down):
    blocks = TOKENS // TOK_DEV
    flat_ids = expert_ids.reshape(blocks, TOK_DEV * 2).astype(jnp.int32)
    onehot = (flat_ids[:, :, None] == jnp.arange(EXPERTS, dtype=jnp.int32)[None, None, :]).astype(jnp.int32)
    slot = jnp.sum((jnp.cumsum(onehot, axis=1) - 1) * onehot, axis=2).astype(jnp.int32)
    position = (flat_ids * CAP + slot).astype(jnp.int32)
    rows_p = jnp.repeat(heads_primal.reshape(blocks, TOK_DEV, FEAT), 2, axis=1)
    rows_t = jnp.repeat(heads_tangent.reshape(blocks, TOK_DEV, FEAT), 2, axis=1)

    def place(where, values):
        return jnp.zeros((EXPERTS * CAP, FEAT), values.dtype).at[where].set(values)

    buf_p = jax.vmap(place)(position, rows_p)
    buf_t = jax.vmap(place)(position, rows_t)
    by_p = buf_p.reshape(blocks, EXPERTS, CAP, FEAT).transpose(1, 0, 2, 3).reshape(EXPERTS, blocks * CAP, FEAT)
    by_t = buf_t.reshape(blocks, EXPERTS, CAP, FEAT).transpose(1, 0, 2, 3).reshape(EXPERTS, blocks * CAP, FEAT)

    def one_expert(packed):
        index, rows, tans = packed
        total_p = jnp.zeros(rows.shape, jnp.float32)
        total_t = jnp.zeros(rows.shape, jnp.float32)
        for half in range(2):
            which = (2 * index + half).astype(jnp.int32)
            gate_w = lax.dynamic_index_in_dim(w_gate, which, 0, keepdims=False)
            up_w = lax.dynamic_index_in_dim(w_up, which, 0, keepdims=False)
            down_w = lax.dynamic_index_in_dim(w_down, which, 0, keepdims=False)
            part_p, part_t = expert_half(rows, tans, gate_w, up_w, down_w)
            total_p = total_p + part_p.astype(jnp.float32)
            total_t = total_t + part_t.astype(jnp.float32)
        return total_p.astype(jnp.bfloat16), total_t.astype(jnp.bfloat16)

    out_p, out_t = lax.map(one_expert, (jnp.arange(EXPERTS, dtype=jnp.int32), by_p, by_t))
    out_p = out_p.reshape(EXPERTS, blocks, CAP, FEAT).transpose(1, 0, 2, 3).reshape(blocks, EXPERTS * CAP, FEAT)
    out_t = out_t.reshape(EXPERTS, blocks, CAP, FEAT).transpose(1, 0, 2, 3).reshape(blocks, EXPERTS * CAP, FEAT)
    got_p = jnp.take_along_axis(out_p, position[:, :, None], axis=1).astype(jnp.float32).reshape(TOKENS, 2, FEAT)
    got_t = jnp.take_along_axis(out_t, position[:, :, None], axis=1).astype(jnp.float32).reshape(TOKENS, 2, FEAT)
    weight = gate_weights[:, :, None]
    slope_w = gate_tangent[:, :, None]
    moe_out = jnp.sum(weight * got_p, axis=1).astype(jnp.bfloat16)
    moe_tangent = jnp.sum(weight * got_t + slope_w * got_p, axis=1).astype(jnp.bfloat16)
    return moe_out, moe_tangent
```

```python
import functools

import jax
import jax.numpy as jnp
from jax import lax
from jax.experimental import pallas as pl
from jax.experimental.pallas import tpu as pltpu
from jax.sharding import PartitionSpec as P

MESH = pl.DeviceIdType.MESH
BF, F32 = jnp.bfloat16, jnp.float32
HOPS = (0, -1, 2, -3)
LANES = 2944
ROWS = 16


def iota(shape, dim):
    return lax.broadcasted_iota(jnp.int32, shape, dim)


def pack_matrix(n, transposed):
    shape = (ROWS * n, ROWS * n)
    a, b = (iota(shape, 1), iota(shape, 0)) if transposed else (iota(shape, 0), iota(shape, 1))
    k, rho = a >> 4, a & 15
    return (b == (rho >> 1) * (2 * n) + k * 2 + (rho & 1)).astype(BF)


def pack_tail(tail, n, out):
    matrix = pack_matrix(n, False)
    for t in range(3):
        groups = 8 if t < 2 else 4
        stacked = jnp.concatenate([tail[:, 128 * (8 * t + j) : 128 * (8 * t + j + 1)] for j in range(groups)], 0)
        out[:, 2560 + 128 * t : 2560 + 128 * (t + 1)] = jnp.dot(
            matrix[:, : groups * 2 * n], stacked, preferred_element_type=F32
        ).astype(BF)


def unpack_tail(messages, n, out):
    matrix = pack_matrix(n, True)
    for t in range(3):
        groups = 8 if t < 2 else 4
        rows = jnp.dot(
            matrix[: groups * 2 * n], messages[:, 2560 + 128 * t : 2560 + 128 * (t + 1)], preferred_element_type=F32
        ).astype(BF)
        for j in range(groups):
            out[:, 128 * (8 * t + j) : 128 * (8 * t + j + 1)] = rows[2 * n * j : 2 * n * (j + 1)]


def layer(
    hp, ht, ids, gates, slopes, w_gate, w_up, w_down, out_p, out_t,
    cols, toks, sbuf, rcv, rsend, rback, gu_own, dn_own, gu_oth, dn_oth, xin, hid, part, tails, wsel,
    own_sem, rg_sem, tk_sem, rt_sem, z_sem, x_sem, c_sem,
):
    seq, ex = lax.axis_index("seq"), lax.axis_index("exp")
    x, c, y, z = seq // 2, lax.rem(seq, 2), ex // 8, lax.rem(ex, 8)
    sgn = 1 - 2 * lax.rem(z, 2)

    def at(xx, cc, yy, zz):
        return (lax.rem(xx + 8, 4) * 2 + lax.rem(cc + 2, 2), lax.rem(yy + 8, 4) * 8 + lax.rem(zz + 16, 8))

    def dest(k):
        return at(x, c, y + k % 4, z + HOPS[k // 4] * sgn)

    def source(k):
        return at(x, c, y - k % 4, z - (k // 4) * sgn)

    partner = at(x, c, y, z + sgn)
    other_core = at(x, 1 - c, y, z)

    def remote(src, dst, send, recv, device):
        return pltpu.make_async_remote_copy(src, dst, send, recv, device_id=device, device_id_type=MESH)

    barrier = pltpu.get_barrier_semaphore()
    for i in range(1, 8):
        pl.semaphore_signal(barrier, inc=1, device_id=(lax.rem(seq + i, 8), ex), device_id_type=MESH)
    for k in range(1, 16):
        pl.semaphore_signal(barrier, inc=1, device_id=dest(k), device_id_type=MESH)
        pl.semaphore_signal(barrier, inc=1, device_id=source(k), device_id_type=MESH)
    pl.semaphore_signal(barrier, inc=1, device_id=partner, device_id_type=MESH)

    own = [
        pltpu.make_async_copy(w.at[0, :, pl.ds(384 * q, 384)], gu_own.at[q, :, pl.ds(384 * g, 384)], own_sem.at[2 * q + g])
        for q in range(4)
        for g, w in enumerate((w_gate, w_up))
    ]
    own.append(pltpu.make_async_copy(w_down.at[0], dn_own, own_sem.at[8]))
    for copy in own:
        copy.start()
    pl.semaphore_wait(barrier, 38)

    def regroup(i, kind):
        to = lax.rem(seq + i, 8)
        heads = (hp, ht)[kind]
        n = 2 * i + kind
        return remote(
            heads.at[pl.ds(pl.multiple_of(to * 128, 128), 128)], cols.at[seq, kind],
            rg_sem.at[0, n], rg_sem.at[1, n], (to, ex),
        )

    for i in range(1, 8):
        for kind in range(2):
            regroup(i, kind).start()
    mine = pl.ds(pl.multiple_of(seq * 128, 128), 128)
    cols[seq, 0] = hp[mine, :]
    cols[seq, 1] = ht[mine, :]

    def region(g, q, core, mine_too):
        if g == 2:
            rows = pl.ds(pl.multiple_of(q * 384 + core * 192, 64), 192)
            return (w_down.at[0, rows] if mine_too else None), dn_oth.at[rows]
        rows = pl.ds(pl.multiple_of(core * 640, 128), 640)
        lanes = pl.ds(pl.multiple_of(q * 384, 128), 384)
        src = (w_gate, w_up)[g].at[0, rows, lanes] if mine_too else None
        return src, gu_oth.at[q, rows, pl.ds(384 * g, 384)]

    def cross(g):
        src, dst = region(g, x, c, True)
        return remote(src, dst, z_sem.at[0, g], z_sem.at[1, g], partner)

    def over_x(g, i):
        _, ref = region(g, x, c, False)
        return remote(ref, ref, x_sem.at[0, 3 * g + i - 1], x_sem.at[1, 3 * g + i - 1], at(x + i, c, y, z))

    def from_x(g, i):
        _, ref = region(g, lax.rem(x - i + 4, 4), c, False)
        return remote(ref, ref, x_sem.at[0, 3 * g + i - 1], x_sem.at[1, 3 * g + i - 1], at(x + i, c, y, z))

    def over_core(g, i, core):
        _, ref = region(g, lax.rem(x - i + 4, 4), core, False)
        return remote(ref, ref, c_sem.at[0, 4 * g + i], c_sem.at[1, 4 * g + i], other_core)

    for g in range(3):
        cross(g).start()

    def row(ref, k):
        return jnp.broadcast_to(ref[:, k : k + 1].astype(F32), (128, 128)).T[:16]

    k16 = iota((16, 128), 0)
    cls = k16 >> 2
    zk = lax.rem(z + sgn * jnp.where(cls == 0, 0, jnp.where(cls == 1, -1, jnp.where(cls == 2, 2, -3))) + 16, 8)
    named = (4 * lax.rem(y + (k16 & 3), 4) + (zk >> 1)).astype(F32)
    first, second = (row(ids, k) == named for k in range(2))
    member = jnp.logical_or(first, second)
    before = (iota((128, 128), 0) < iota((128, 128), 1)).astype(BF)
    rank = jnp.dot(member.astype(BF), before, preferred_element_type=F32)
    values = [jnp.where(member, rank, -1.0).astype(BF)]
    for ref in (gates, slopes):
        weight = jnp.where(first, row(ref, 0), jnp.where(second, row(ref, 1), 0.0))
        high = weight.astype(BF)
        values += [high, (weight - high.astype(F32)).astype(BF)]
    slot_row = iota((288, 16), 0)
    spread = (jnp.where(slot_row < 256, slot_row >> 4, (slot_row - 256) >> 1) == iota((288, 16), 1)).astype(BF)
    spread = jnp.dot(spread, jnp.concatenate(values, 1), preferred_element_type=F32)
    a = iota((288, 128), 0)
    chosen = spread[:, :128] == jnp.where(a < 256, a & 15, 16 + (a & 1)).astype(F32)
    for i, part_of in enumerate((1, 3, 2, 4)):
        wsel[i // 2, :, 128 * (i % 2) : 128 * (i % 2 + 1)] = jnp.where(
            chosen, spread[:, 128 * part_of : 128 * (part_of + 1)], 0.0
        ).astype(BF)
    chosen = chosen.astype(BF)

    for i in range(1, 8):
        for kind in range(2):
            regroup(i, kind).wait_recv()
    for half in range(2):
        for kind in range(2):
            total = jnp.zeros((128, 640), F32)
            for q in range(4):
                place = (iota((160, 640), 1) == iota((160, 640), 0) + 160 * q).astype(BF)
                total += jnp.dot(cols[4 * half + q, kind], place, preferred_element_type=F32)
            toks[:, 1280 * kind + 640 * half : 1280 * kind + 640 * (half + 1)] = total.astype(BF)
    sbuf[:, :2560] = jnp.dot(chosen[:256], toks[...], preferred_element_type=F32).astype(BF)
    pack_tail(jnp.dot(chosen[256:], toks[...], preferred_element_type=F32).astype(BF), 16, sbuf)

    def rows_of(k):
        return pl.ds(ROWS * k, ROWS)

    def token(k):
        return remote(sbuf.at[rows_of(k)], rcv.at[rows_of(k)], tk_sem.at[0, k], tk_sem.at[1, k], dest(k))

    def give_back(k):
        return remote(rsend.at[rows_of(k)], rback.at[rows_of(k)], rt_sem.at[0, k], rt_sem.at[1, k], source(k))

    for j in range(4):
        for d in (3, 2, 1, 0):
            if d or j:
                token(4 * d + j).start()
    rcv[:ROWS] = sbuf[:ROWS]

    def hidden(b, weights):
        @pl.loop(0, 4)
        def _(q):
            both = jnp.dot(xin[b], weights[q], preferred_element_type=F32)
            pre_gate, tan_gate = both[:144, :384], both[144:, :384]
            pre_up, tan_up = both[:144, 384:], both[144:, 384:]
            sigma = jax.nn.sigmoid(pre_gate)
            swish = pre_gate * sigma
            slope = sigma * (1.0 + pre_gate * (1.0 - sigma))
            lanes = pl.ds(pl.multiple_of(q * 384, 128), 384)
            hid[b, :144, lanes] = (swish * pre_up).astype(BF)
            hid[b, 144:, lanes] = (slope * tan_gate * pre_up + swish * tan_up).astype(BF)

    def arrive(g):
        cross(g).wait_recv()
        for i in (1, 3, 2):
            over_x(g, i).start()
        over_core(g, 0, c).start()

    def pass_on(g):
        for i in (1, 3, 2):
            from_x(g, i).wait_recv()
            over_core(g, i, c).start()

    def own_half(b):
        for k in range(8 * b, 8 * b + 8):
            if k:
                token(k).wait_recv()
        here = rcv.at[128 * b : 128 * (b + 1)]
        unpack_tail(here, 8, tails)
        for kind in range(2):
            xin[b, 144 * kind : 144 * kind + 128] = here[:, 1280 * kind : 1280 * (kind + 1)]
            xin[b, 144 * kind + 128 : 144 * (kind + 1)] = tails[:, 1280 * kind : 1280 * (kind + 1)]
        hidden(b, gu_own)
        part[b] = jnp.dot(hid[b], dn_own[...], preferred_element_type=F32).astype(BF)

    for copy in own:
        copy.wait()
    arrive(0)
    arrive(1)
    pass_on(0)
    arrive(2)
    own_half(0)
    pass_on(1)
    own_half(1)
    for g in range(2):
        for i in range(4):
            over_core(g, i, 1 - c).wait_recv()
    hidden(1, gu_oth)
    hidden(0, gu_oth)
    pass_on(2)
    for i in range(4):
        over_core(2, i, 1 - c).wait_recv()
    for b in (1, 0):
        here = jnp.dot(hid[b], dn_oth[...], preferred_element_type=F32).astype(BF)
        total = (here.astype(F32) + part[b].astype(F32)).astype(BF)
        out = rsend.at[128 * b : 128 * (b + 1)]
        for kind in range(2):
            out[:, 1280 * kind : 1280 * (kind + 1)] = total[144 * kind : 144 * kind + 128]
        pack_tail(jnp.concatenate([total[128:144], total[272:288]], 1), 8, out)
        for k in (15, 14, 13, 12, 11, 10, 9, 8) if b else (7, 6, 5, 4, 3, 2, 1):
            give_back(k).start()
    rback[:ROWS] = rsend[:ROWS]
    for k in range(1, 16):
        give_back(k).wait_recv()

    unpack_tail(rback, 16, toks.at[:32])

    def combine(side, main_lanes, width):
        total = jnp.zeros((width, 1280), F32)
        for i in range(2):
            total += lax.dot_general(
                wsel[i, :256, :width], rback[:, main_lanes], (((0,), (0,)), ((), ())), preferred_element_type=F32
            )
            total += lax.dot_general(
                wsel[i, 256:, :width], toks[:32, main_lanes], (((0,), (0,)), ((), ())), preferred_element_type=F32
            )
        return total

    from_p = combine(0, slice(0, 1280), 256)
    out_p[...] = from_p[:128].astype(BF)
    out_t[...] = (combine(1, slice(1280, 2560), 128) + from_p[128:]).astype(BF)

    for i in range(1, 8):
        for kind in range(2):
            regroup(i, kind).wait_send()
    for k in range(1, 16):
        token(k).wait_send()
        give_back(k).wait_send()
    for g in range(3):
        cross(g).wait_send()
        for i in range(1, 4):
            over_x(g, i).wait_send()
        for i in range(4):
            over_core(g, i, c).wait_send()


def per_device(*args):
    vmem, hbm = pl.BlockSpec(memory_space=pltpu.VMEM), pl.BlockSpec(memory_space=pl.ANY)
    dma = pltpu.SemaphoreType.DMA
    return pl.pallas_call(
        layer,
        out_shape=(jax.ShapeDtypeStruct((128, 1280), BF),) * 2,
        in_specs=[vmem] * 5 + [hbm] * 3,
        out_specs=(vmem, vmem),
        scratch_shapes=[
            pltpu.VMEM((8, 2, 128, 160), BF),
            pltpu.VMEM((128, 2560), BF),
            pltpu.VMEM((256, LANES), BF),
            pltpu.VMEM((256, LANES), BF),
            pltpu.VMEM((256, LANES), BF),
            pltpu.VMEM((256, LANES), BF),
            pltpu.VMEM((4, 1280, 768), BF),
            pltpu.VMEM((1536, 1280), BF),
            pltpu.VMEM((4, 1280, 768), BF),
            pltpu.VMEM((1536, 1280), BF),
            pltpu.VMEM((2, 288, 1280), BF),
            pltpu.VMEM((2, 288, 1536), BF),
            pltpu.VMEM((2, 288, 1280), BF),
            pltpu.VMEM((16, 2560), BF),
            pltpu.VMEM((2, 288, 256), BF),
            dma((9,)),
            dma((2, 16)),
            dma((2, 16)),
            dma((2, 16)),
            dma((2, 3)),
            dma((2, 9)),
            dma((2, 12)),
        ],
        compiler_params=pltpu.CompilerParams(
            collective_id=0, has_side_effects=True, vmem_limit_bytes=60 << 20
        ),
    )(*args)


def solution(mesh):
    tokens = P(("exp", "seq"), None)
    halves = P("exp", None, None)
    return jax.shard_map(
        per_device,
        mesh=mesh,
        in_specs=(P("exp", "seq"), P("exp", "seq"), tokens, tokens, tokens, halves, halves, halves),
        out_specs=(tokens, tokens),
        check_vma=False,
    )
```

```python
import functools

import jax
import jax.numpy as jnp
from jax import lax
from jax.experimental import pallas as pl
from jax.experimental.pallas import tpu as pltpu
from jax.sharding import PartitionSpec as P

MESH = pl.DeviceIdType.MESH
BF, F32 = jnp.bfloat16, jnp.float32
HOPS = (0, -1, 2, -3)
LANES = 2944
ROWS = 16
CHUNKS = 6


def iota(shape, dim):
    return lax.broadcasted_iota(jnp.int32, shape, dim)


def pack_matrix(n, transposed):
    shape = (ROWS * n, ROWS * n)
    a, b = (iota(shape, 1), iota(shape, 0)) if transposed else (iota(shape, 0), iota(shape, 1))
    k, rho = a >> 4, a & 15
    return (b == (rho >> 1) * (2 * n) + k * 2 + (rho & 1)).astype(BF)


def pack_tail(tail, n, out):
    matrix = pack_matrix(n, False)
    for t in range(3):
        groups = 8 if t < 2 else 4
        stacked = jnp.concatenate([tail[:, 128 * (8 * t + j) : 128 * (8 * t + j + 1)] for j in range(groups)], 0)
        out[:, 2560 + 128 * t : 2560 + 128 * (t + 1)] = jnp.dot(
            matrix[:, : groups * 2 * n], stacked, preferred_element_type=F32
        ).astype(BF)


def unpack_tail(messages, n, out):
    matrix = pack_matrix(n, True)
    for t in range(3):
        groups = 8 if t < 2 else 4
        rows = jnp.dot(
            matrix[: groups * 2 * n], messages[:, 2560 + 128 * t : 2560 + 128 * (t + 1)], preferred_element_type=F32
        ).astype(BF)
        for j in range(groups):
            out[:, 128 * (8 * t + j) : 128 * (8 * t + j + 1)] = rows[2 * n * j : 2 * n * (j + 1)]


def layer(
    hp, ht, ids, gates, slopes, w_gate, w_up, w_down, out,
    toks, sbuf, rcv, rsend, rback, gu_own, dn_own, gu_oth, dn_oth, xin, hid, part, tails, wsel,
    own_sem, rg_sem, tk_sem, rt_sem, z_sem, x_sem, r_sem, c_sem, plane_sem,
):
    seq, ex = lax.axis_index("seq"), lax.axis_index("exp")
    x, c, y, z = seq // 2, lax.rem(seq, 2), ex // 8, lax.rem(ex, 8)
    sgn = 1 - 2 * lax.rem(z, 2)

    ys = [lax.rem(y + j, 4) * 8 for j in range(4)]
    around = [lax.rem(z + 8 + hop * sgn, 8) for hop in (0, 1, 2, -1, -2, -3)]
    xs = [lax.rem(x + i, 4) for i in range(4)]

    def dest(k):
        return (seq, ys[k % 4] + around[(0, 3, 2, 5)[k // 4]])

    def source(k):
        return (seq, ys[-k % 4] + around[(0, 3, 4, 5)[k // 4]])

    partner = (seq, ys[0] + around[1])
    other_core = (2 * x + 1 - c, ex)

    def remote(src, dst, send, recv, device):
        return pltpu.make_async_remote_copy(src, dst, send, recv, device_id=device, device_id_type=MESH)

    barrier = pltpu.get_barrier_semaphore()
    for i in range(1, 8):
        pl.semaphore_signal(barrier, inc=1, device_id=(lax.rem(seq + i, 8), ex), device_id_type=MESH)
    for i in range(1, 8):
        pl.semaphore_signal(barrier, inc=1, device_id=(seq, ys[0] + lax.rem(z + i, 8)), device_id_type=MESH)
    for j in range(1, 4):
        pl.semaphore_signal(barrier, inc=1, device_id=(seq, ys[j] + z), device_id_type=MESH)

    own = [
        pltpu.make_async_copy(w.at[0, :, pl.ds(384 * q, 384)], gu_own.at[q, :, pl.ds(384 * g, 384)], own_sem.at[2 * q + g])
        for q in range(4)
        for g, w in enumerate((w_gate, w_up))
    ]
    own.append(pltpu.make_async_copy(w_down.at[0], dn_own, own_sem.at[8]))
    pl.semaphore_wait(barrier, 17)

    def regroup(i, kind):
        to = lax.rem(seq + i, 8)
        n = 2 * i + kind
        src = (hp, ht)[kind].at[:, pl.ds(pl.multiple_of(to * 128, 128), 128)]
        dst = toks.at[kind, pl.ds(pl.multiple_of(seq * 160, 32), 160)]
        if i == 0:
            return pltpu.make_async_copy(src, dst, rg_sem.at[1, n])
        return remote(src, dst, rg_sem.at[0, n], rg_sem.at[1, n], (to, ex))

    for kind in range(2):
        for i in range(8):
            regroup(i, kind).start()

    def region(n, q, core, half=None, source=False):
        g, sub = n // 2, n % 2
        size = 320 if g < 2 else 96
        first = core * (2 * size) + sub * size
        if half is not None:
            size //= 2
            first += half * size
        if g == 2:
            rows = pl.ds(pl.multiple_of(q * 384 + first, 16), size)
            return w_down.at[0, rows] if source else dn_oth.at[rows]
        rows = pl.ds(pl.multiple_of(first, 16), size)
        if source:
            return (w_gate, w_up)[g].at[0, rows, pl.ds(pl.multiple_of(q * 384, 128), 384)]
        return gu_oth.at[q, rows, pl.ds(384 * g, 384)]

    def cross(n):
        return remote(region(n, x, c, source=True), region(n, x, c), z_sem.at[0, n], z_sem.at[1, n], partner)

    def along(ref, sems, n, step):
        i = 2 * n + (step < 0)
        return remote(ref, ref, sems.at[0, i], sems.at[1, i], (2 * xs[step % 4] + c, ex))

    def send_x(n, step):
        return along(region(n, x, c), x_sem, n, step)

    def recv_x(n, step):
        return along(region(n, xs[-step % 4], c), x_sem, n, step)

    def send_on(n, step):
        return along(region(n, xs[-step % 4], c, half=int(step < 0)), r_sem, n, step)

    def recv_on(n, step):
        return along(region(n, xs[2], c, half=int(step < 0)), r_sem, n, step)

    def over_core(n, i, core):
        ref = region(n, xs[(0, 3, 1, 2)[i]], core)
        return remote(ref, ref, c_sem.at[0, 4 * n + i], c_sem.at[1, 4 * n + i], other_core)

    for n in range(CHUNKS):
        cross(n).start()
    for j in range(1, 4):
        pl.semaphore_signal(plane_sem, inc=1, device_id=(seq, ys[j] + z), device_id_type=MESH)
    for copy in own:
        copy.start()

    def row(ref, k):
        return jnp.broadcast_to(ref[k : k + 1, :].astype(F32), (16, 128))

    k16 = iota((16, 128), 0)
    cls = k16 >> 2
    zk = lax.rem(z + sgn * jnp.where(cls == 0, 0, jnp.where(cls == 1, -1, jnp.where(cls == 2, 2, -3))) + 16, 8)
    named = (4 * lax.rem(y + (k16 & 3), 4) + (zk >> 1)).astype(F32)
    first, second = (row(ids, k) == named for k in range(2))
    member = jnp.logical_or(first, second)
    before = (iota((128, 128), 0) < iota((128, 128), 1)).astype(BF)
    rank = jnp.dot(member.astype(BF), before, preferred_element_type=F32)
    values = [jnp.where(member, rank, -1.0).astype(BF)]
    for ref in (gates, slopes):
        weight = jnp.where(first, row(ref, 0), jnp.where(second, row(ref, 1), 0.0))
        high = weight.astype(BF)
        values += [high, (weight - high.astype(F32)).astype(BF)]
    slot_row = iota((288, 16), 0)
    spread = (jnp.where(slot_row < 256, slot_row >> 4, (slot_row - 256) >> 1) == iota((288, 16), 1)).astype(BF)
    spread = jnp.dot(spread, jnp.concatenate(values, 1), preferred_element_type=F32)
    a = iota((288, 128), 0)
    chosen = spread[:, :128] == jnp.where(a < 256, a & 15, 16 + (a & 1)).astype(F32)
    for i, part_of in enumerate((1, 3, 2, 4)):
        wsel[i // 2, :, 128 * (i % 2) : 128 * (i % 2 + 1)] = jnp.where(
            chosen, spread[:, 128 * part_of : 128 * (part_of + 1)], 0.0
        ).astype(BF)
    chosen = chosen.astype(BF)

    def arrive(n):
        cross(n).wait_recv()
        for step in (1, -1):
            send_x(n, step).start()
        over_core(n, 0, c).start()

    def pass_on(n):
        for i, step in ((1, 1), (2, -1)):
            recv_x(n, step).wait_recv()
            send_on(n, step).start()
            over_core(n, i, c).start()

    def finish(n):
        for step in (1, -1):
            recv_on(n, step).wait_recv()
        over_core(n, 3, c).start()

    arrive(0)
    for kind in range(2):
        regroup(0, kind).wait()
        for i in range(1, 8):
            regroup(i, kind).wait_recv()

    def dispatch(rows, kind):
        return lax.dot_general(
            rows, toks[kind], (((1,), (1,)), ((), ())), preferred_element_type=F32
        ).astype(BF)

    for kind in range(2):
        sbuf[:, 1280 * kind : 1280 * (kind + 1)] = dispatch(chosen[:256], kind)
    pack_tail(jnp.concatenate([dispatch(chosen[256:], kind) for kind in range(2)], 1), 16, sbuf)

    def rows_of(k):
        return pl.ds(ROWS * k, ROWS)

    def token(k):
        return remote(sbuf.at[rows_of(k)], rcv.at[rows_of(k)], tk_sem.at[0, k], tk_sem.at[1, k], dest(k))

    def give_back(k):
        return remote(rsend.at[rows_of(k)], rback.at[rows_of(k)], rt_sem.at[0, k], rt_sem.at[1, k], source(k))

    pl.semaphore_wait(plane_sem, 3)
    for first in (0, 2):
        for j in range(4):
            for d in (first + 1, first):
                if d or j:
                    token(4 * d + j).start()
    rcv[:ROWS] = sbuf[:ROWS]

    def hidden(b, weights):
        @pl.loop(0, 4)
        def _(q):
            both = jnp.dot(xin[b], weights[q], preferred_element_type=F32)
            pre_gate, tan_gate = both[:144, :384], both[144:, :384]
            pre_up, tan_up = both[:144, 384:], both[144:, 384:]
            sigma = jax.nn.sigmoid(pre_gate)
            swish = pre_gate * sigma
            slope = sigma * (1.0 + pre_gate * (1.0 - sigma))
            lanes = pl.ds(pl.multiple_of(q * 384, 128), 384)
            hid[b, :144, lanes] = (swish * pre_up).astype(BF)
            hid[b, 144:, lanes] = (slope * tan_gate * pre_up + swish * tan_up).astype(BF)

    def own_half(b):
        for k in range(8 * b, 8 * b + 8):
            if k:
                token(k).wait_recv()
        here = rcv.at[128 * b : 128 * (b + 1)]
        unpack_tail(here, 8, tails)
        for kind in range(2):
            xin[b, 144 * kind : 144 * kind + 128] = here[:, 1280 * kind : 1280 * (kind + 1)]
            xin[b, 144 * kind + 128 : 144 * (kind + 1)] = tails[:, 1280 * kind : 1280 * (kind + 1)]
        hidden(b, gu_own)
        part[b] = jnp.dot(hid[b], dn_own[...], preferred_element_type=F32).astype(BF)

    arrive(1)
    pass_on(0)
    arrive(2)
    pass_on(1)
    finish(0)
    arrive(3)
    for copy in own:
        copy.wait()
    own_half(0)
    pass_on(2)
    finish(1)
    arrive(4)
    pass_on(3)
    finish(2)
    arrive(5)
    finish(3)
    for n in range(4):
        for i in range(4):
            over_core(n, i, 1 - c).wait_recv()
    hidden(0, gu_oth)
    pass_on(4)
    own_half(1)
    pass_on(5)
    finish(4)
    hidden(1, gu_oth)
    finish(5)
    for n in range(4, CHUNKS):
        for i in range(4):
            over_core(n, i, 1 - c).wait_recv()
    for b in (1, 0):
        here = jnp.dot(hid[b], dn_oth[...], preferred_element_type=F32).astype(BF)
        total = (here.astype(F32) + part[b].astype(F32)).astype(BF)
        back = rsend.at[128 * b : 128 * (b + 1)]
        for kind in range(2):
            back[:, 1280 * kind : 1280 * (kind + 1)] = total[144 * kind : 144 * kind + 128]
        pack_tail(jnp.concatenate([total[128:144], total[272:288]], 1), 8, back)
        for k in (15, 14, 13, 12, 11, 10, 9, 8) if b else (7, 6, 5, 4, 3, 2, 1):
            give_back(k).start()
    rback[:ROWS] = rsend[:ROWS]

    def combine(total, b, kind, width):
        lanes = slice(1280 * kind, 1280 * (kind + 1))
        for i in range(2):
            for rows, held in (
                (slice(128 * b, 128 * (b + 1)), rback[128 * b : 128 * (b + 1), lanes]),
                (slice(256 + 16 * b, 256 + 16 * (b + 1)), tails[:, lanes]),
            ):
                total += lax.dot_general(
                    wsel[i, rows, :width], held, (((0,), (0,)), ((), ())), preferred_element_type=F32
                )
        return total

    from_p, from_t = jnp.zeros((256, 1280), F32), jnp.zeros((128, 1280), F32)
    for b in (1, 0):
        for k in range(8 * b, 8 * b + 8):
            if k:
                give_back(k).wait_recv()
        unpack_tail(rback.at[128 * b : 128 * (b + 1)], 8, tails)
        from_p = combine(from_p, b, 0, 256)
        from_t = combine(from_t, b, 1, 128)
    out[:128] = from_p[:128].astype(BF)
    out[128:] = (from_t + from_p[128:]).astype(BF)

    for i in range(1, 8):
        for kind in range(2):
            regroup(i, kind).wait_send()
    for k in range(1, 16):
        token(k).wait_send()
        give_back(k).wait_send()
    for n in range(CHUNKS):
        cross(n).wait_send()
        for step in (1, -1):
            send_x(n, step).wait_send()
            send_on(n, step).wait_send()
        for i in range(4):
            over_core(n, i, c).wait_send()


def split(both, out_p, out_t):
    out_p[...] = both[:128]
    out_t[...] = both[128:]


def per_device(*args):
    args = [a.T for a in args[:5]] + list(args[5:])
    vmem, hbm = pl.BlockSpec(memory_space=pltpu.VMEM), pl.BlockSpec(memory_space=pl.ANY)
    dma = pltpu.SemaphoreType.DMA
    both = pl.pallas_call(
        layer,
        out_shape=jax.ShapeDtypeStruct((256, 1280), BF),
        in_specs=[hbm] * 2 + [vmem] * 3 + [hbm] * 3,
        out_specs=vmem,
        scratch_shapes=[
            pltpu.VMEM((2, 1280, 128), BF),
            pltpu.VMEM((256, LANES), BF),
            pltpu.VMEM((256, LANES), BF),
            pltpu.VMEM((256, LANES), BF),
            pltpu.VMEM((256, LANES), BF),
            pltpu.VMEM((4, 1280, 768), BF),
            pltpu.VMEM((1536, 1280), BF),
            pltpu.VMEM((4, 1280, 768), BF),
            pltpu.VMEM((1536, 1280), BF),
            pltpu.VMEM((2, 288, 1280), BF),
            pltpu.VMEM((2, 288, 1536), BF),
            pltpu.VMEM((2, 288, 1280), BF),
            pltpu.VMEM((16, 2560), BF),
            pltpu.VMEM((2, 288, 256), BF),
            dma((9,)),
            dma((2, 16)),
            dma((2, 16)),
            dma((2, 16)),
            dma((2, CHUNKS)),
            dma((2, 2 * CHUNKS)),
            dma((2, 2 * CHUNKS)),
            dma((2, 4 * CHUNKS)),
            pltpu.SemaphoreType.REGULAR,
        ],
        compiler_params=pltpu.CompilerParams(
            collective_id=0, has_side_effects=True, vmem_limit_bytes=60 << 20
        ),
    )(*args)
    return pl.pallas_call(split, out_shape=(jax.ShapeDtypeStruct((128, 1280), BF),) * 2)(both)


def solution(mesh):
    tokens = P(("exp", "seq"), None)
    halves = P("exp", None, None)
    return jax.shard_map(
        per_device,
        mesh=mesh,
        in_specs=(P("exp", "seq"), P("exp", "seq"), tokens, tokens, tokens, halves, halves, halves),
        out_specs=(tokens, tokens),
        check_vma=False,
    )
```

```python
import functools

import jax
import jax.numpy as jnp
from jax import lax
from jax.experimental import pallas as pl
from jax.experimental.pallas import tpu as pltpu
from jax.sharding import PartitionSpec as P

MESH = pl.DeviceIdType.MESH
BF, F32 = jnp.bfloat16, jnp.float32
HOPS = (0, -1, 2, -3)
LANES = 2944
ROWS = 16
CHUNKS = 6


def iota(shape, dim):
    return lax.broadcasted_iota(jnp.int32, shape, dim)


def pack_matrix(n, transposed):
    shape = (ROWS * n, ROWS * n)
    a, b = (iota(shape, 1), iota(shape, 0)) if transposed else (iota(shape, 0), iota(shape, 1))
    k, rho = a >> 4, a & 15
    return (b == (rho >> 1) * (2 * n) + k * 2 + (rho & 1)).astype(BF)


def pack_tail(tail, n, out):
    matrix = pack_matrix(n, False)
    for t in range(3):
        groups = 8 if t < 2 else 4
        stacked = jnp.concatenate([tail[:, 128 * (8 * t + j) : 128 * (8 * t + j + 1)] for j in range(groups)], 0)
        out[:, 2560 + 128 * t : 2560 + 128 * (t + 1)] = jnp.dot(
            matrix[:, : groups * 2 * n], stacked, preferred_element_type=F32
        ).astype(BF)


def unpack_tail(messages, n, out):
    matrix = pack_matrix(n, True)
    for t in range(3):
        groups = 8 if t < 2 else 4
        rows = jnp.dot(
            matrix[: groups * 2 * n], messages[:, 2560 + 128 * t : 2560 + 128 * (t + 1)], preferred_element_type=F32
        ).astype(BF)
        for j in range(groups):
            out[:, 128 * (8 * t + j) : 128 * (8 * t + j + 1)] = rows[2 * n * j : 2 * n * (j + 1)]


def layer(
    hp, ht, ids, gates, slopes, w_gate, w_up, w_down, out,
    toks, sbuf, rcv, rsend, rback, gu_own, dn_own, gu_oth, dn_oth, xin, hid, part, tails, wsel,
    own_sem, rg_sem, tk_sem, rt_sem, z_sem, x_sem, r_sem, c_sem, plane_sem,
):
    seq, ex = lax.axis_index("seq"), lax.axis_index("exp")
    x, c, y, z = seq // 2, lax.rem(seq, 2), ex // 8, lax.rem(ex, 8)
    sgn = 1 - 2 * lax.rem(z, 2)

    ys = [lax.rem(y + j, 4) * 8 for j in range(4)]
    around = [lax.rem(z + 8 + hop * sgn, 8) for hop in (0, 1, 2, -1, -2, -3)]
    xs = [lax.rem(x + i, 4) for i in range(4)]

    def dest(k):
        return (seq, ys[k % 4] + around[(0, 3, 2, 5)[k // 4]])

    def source(k):
        return (seq, ys[-k % 4] + around[(0, 3, 4, 5)[k // 4]])

    partner = (seq, ys[0] + around[1])
    other_core = (2 * x + 1 - c, ex)

    def remote(src, dst, send, recv, device):
        return pltpu.make_async_remote_copy(src, dst, send, recv, device_id=device, device_id_type=MESH)

    barrier = pltpu.get_barrier_semaphore()
    for i in range(1, 8):
        pl.semaphore_signal(barrier, inc=1, device_id=(lax.rem(seq + i, 8), ex), device_id_type=MESH)
    for i in range(1, 8):
        pl.semaphore_signal(barrier, inc=1, device_id=(seq, ys[0] + lax.rem(z + i, 8)), device_id_type=MESH)
    for j in range(1, 4):
        pl.semaphore_signal(barrier, inc=1, device_id=(seq, ys[j] + z), device_id_type=MESH)

    own = [
        pltpu.make_async_copy(w.at[0, :, pl.ds(384 * q, 384)], gu_own.at[q, :, pl.ds(384 * g, 384)], own_sem.at[2 * q + g])
        for q in range(4)
        for g, w in enumerate((w_gate, w_up))
    ]
    own.append(pltpu.make_async_copy(w_down.at[0], dn_own, own_sem.at[8]))
    pl.semaphore_wait(barrier, 17)

    def regroup(i, kind):
        to = lax.rem(seq + i, 8)
        n = 2 * i + kind
        src = (hp, ht)[kind].at[:, pl.ds(pl.multiple_of(to * 128, 128), 128)]
        dst = toks.at[kind, pl.ds(pl.multiple_of(seq * 160, 32), 160)]
        if i == 0:
            return pltpu.make_async_copy(src, dst, rg_sem.at[1, n])
        return remote(src, dst, rg_sem.at[0, n], rg_sem.at[1, n], (to, ex))

    for kind in range(2):
        for i in range(8):
            regroup(i, kind).start()

    def region(n, q, core, half=None, source=False):
        g, sub = n // 2, n % 2
        size = 320 if g < 2 else 96
        first = core * (2 * size) + sub * size
        if half is not None:
            size //= 2
            first += half * size
        if g == 2:
            rows = pl.ds(pl.multiple_of(q * 384 + first, 16), size)
            return w_down.at[0, rows] if source else dn_oth.at[rows]
        rows = pl.ds(pl.multiple_of(first, 16), size)
        if source:
            return (w_gate, w_up)[g].at[0, rows, pl.ds(pl.multiple_of(q * 384, 128), 384)]
        return gu_oth.at[q, rows, pl.ds(384 * g, 384)]

    def cross(n):
        return remote(region(n, x, c, source=True), region(n, x, c), z_sem.at[0, n], z_sem.at[1, n], partner)

    def along(ref, sems, n, step):
        i = 2 * n + (step < 0)
        return remote(ref, ref, sems.at[0, i], sems.at[1, i], (2 * xs[step % 4] + c, ex))

    def send_x(n, step):
        return along(region(n, x, c), x_sem, n, step)

    def recv_x(n, step):
        return along(region(n, xs[-step % 4], c), x_sem, n, step)

    def send_on(n, step):
        return along(region(n, xs[-step % 4], c, half=int(step < 0)), r_sem, n, step)

    def recv_on(n, step):
        return along(region(n, xs[2], c, half=int(step < 0)), r_sem, n, step)

    def over_core(n, i, core):
        ref = region(n, xs[(0, 3, 1, 2)[i]], core)
        return remote(ref, ref, c_sem.at[0, 4 * n + i], c_sem.at[1, 4 * n + i], other_core)

    for n in range(CHUNKS):
        cross(n).start()
    for j in range(1, 4):
        pl.semaphore_signal(plane_sem, inc=1, device_id=(seq, ys[j] + z), device_id_type=MESH)
    for copy in own:
        copy.start()

    def row(ref, k):
        return jnp.broadcast_to(ref[k : k + 1, :].astype(F32), (16, 128))

    k16 = iota((16, 128), 0)
    cls = k16 >> 2
    zk = lax.rem(z + sgn * jnp.where(cls == 0, 0, jnp.where(cls == 1, -1, jnp.where(cls == 2, 2, -3))) + 16, 8)
    named = (4 * lax.rem(y + (k16 & 3), 4) + (zk >> 1)).astype(F32)
    first, second = (row(ids, k) == named for k in range(2))
    member = jnp.logical_or(first, second)
    before = (iota((128, 128), 0) < iota((128, 128), 1)).astype(BF)
    rank = jnp.dot(member.astype(BF), before, preferred_element_type=F32)
    values = [jnp.where(member, rank, -1.0).astype(BF)]
    for ref in (gates, slopes):
        weight = jnp.where(first, row(ref, 0), jnp.where(second, row(ref, 1), 0.0))
        high = weight.astype(BF)
        values += [high, (weight - high.astype(F32)).astype(BF)]
    slot_row = iota((288, 16), 0)
    spread = (jnp.where(slot_row < 256, slot_row >> 4, (slot_row - 256) >> 1) == iota((288, 16), 1)).astype(BF)
    spread = jnp.dot(spread, jnp.concatenate(values, 1), preferred_element_type=F32)
    a = iota((288, 128), 0)
    chosen = spread[:, :128] == jnp.where(a < 256, a & 15, 16 + (a & 1)).astype(F32)
    for i, part_of in enumerate((1, 3, 2, 4)):
        wsel[i // 2, :, 128 * (i % 2) : 128 * (i % 2 + 1)] = jnp.where(
            chosen, spread[:, 128 * part_of : 128 * (part_of + 1)], 0.0
        ).astype(BF)
    chosen = chosen.astype(BF)

    def arrive(n):
        cross(n).wait_recv()
        for step in (1, -1):
            send_x(n, step).start()
        over_core(n, 0, c).start()

    def pass_on(n):
        for i, step in ((1, 1), (2, -1)):
            recv_x(n, step).wait_recv()
            send_on(n, step).start()
            over_core(n, i, c).start()

    def finish(n):
        for step in (1, -1):
            recv_on(n, step).wait_recv()
        over_core(n, 3, c).start()

    def regrouped():
        for kind in range(2):
            regroup(0, kind).wait()
            for i in range(1, 8):
                regroup(i, kind).wait_recv()

    def dispatch(rows, kind):
        return lax.dot_general(
            rows, toks[kind], (((1,), (1,)), ((), ())), preferred_element_type=F32
        ).astype(BF)

    def rows_of(k):
        return pl.ds(ROWS * k, ROWS)

    def token(k):
        return remote(sbuf.at[rows_of(k)], rcv.at[rows_of(k)], tk_sem.at[0, k], tk_sem.at[1, k], dest(k))

    def give_back(k):
        return remote(rsend.at[rows_of(k)], rback.at[rows_of(k)], rt_sem.at[0, k], rt_sem.at[1, k], source(k))

    def send_rows():
        for kind in range(2):
            sbuf[:, 1280 * kind : 1280 * (kind + 1)] = dispatch(chosen[:256], kind)
        pack_tail(jnp.concatenate([dispatch(chosen[256:], kind) for kind in range(2)], 1), 16, sbuf)
        pl.semaphore_wait(plane_sem, 3)
        for first in (0, 2):
            for j in range(4):
                for d in (first + 1, first):
                    if d or j:
                        token(4 * d + j).start()
        rcv[:ROWS] = sbuf[:ROWS]

    def hidden(b, weights):
        @pl.loop(0, 4, unroll=2)
        def _(q):
            both = jnp.dot(xin[b], weights[q], preferred_element_type=F32)
            pre_gate, tan_gate = both[:144, :384], both[144:, :384]
            pre_up, tan_up = both[:144, 384:], both[144:, 384:]
            sigma = jax.nn.sigmoid(pre_gate)
            swish = pre_gate * sigma
            slope = sigma * (1.0 + pre_gate * (1.0 - sigma))
            lanes = pl.ds(pl.multiple_of(q * 384, 128), 384)
            hid[b, :144, lanes] = (swish * pre_up).astype(BF)
            hid[b, 144:, lanes] = (slope * tan_gate * pre_up + swish * tan_up).astype(BF)

    def rows_in(b):
        for k in range(8 * b, 8 * b + 8):
            if k:
                token(k).wait_recv()
        here = rcv.at[128 * b : 128 * (b + 1)]
        unpack_tail(here, 8, tails)
        for kind in range(2):
            xin[b, 144 * kind : 144 * kind + 128] = here[:, 1280 * kind : 1280 * (kind + 1)]
            xin[b, 144 * kind + 128 : 144 * (kind + 1)] = tails[:, 1280 * kind : 1280 * (kind + 1)]

    def own_hidden(b):
        hidden(b, gu_own)

    def own_down(b):
        part[b] = jnp.dot(hid[b], dn_own[...], preferred_element_type=F32).astype(BF)

    def other_hidden(b):
        hidden(b, gu_oth)

    def own_here():
        for copy in own:
            copy.wait()

    def from_core(n):
        for i in range(4):
            over_core(n, i, 1 - c).wait_recv()

    order = (
        (arrive, 0), (regrouped,), (send_rows,), (arrive, 1), (pass_on, 0), (arrive, 2),
        (pass_on, 1), (finish, 0), (arrive, 3), (pass_on, 2), (finish, 1), (own_here,),
        (rows_in, 0), (own_hidden, 0), (arrive, 4), (pass_on, 3), (finish, 2), (own_down, 0),
        (arrive, 5), (pass_on, 4), (finish, 3), (from_core, 0), (from_core, 1), (from_core, 2),
        (from_core, 3), (other_hidden, 0), (rows_in, 1), (own_hidden, 1), (pass_on, 5), (finish, 4),
        (own_down, 1), (other_hidden, 1), (finish, 5), (from_core, 4), (from_core, 5),
    )
    for step, *arg in order:
        step(*arg)
    for b in (1, 0):
        here = jnp.dot(hid[b], dn_oth[...], preferred_element_type=F32).astype(BF)
        total = (here.astype(F32) + part[b].astype(F32)).astype(BF)
        back = rsend.at[128 * b : 128 * (b + 1)]
        for kind in range(2):
            back[:, 1280 * kind : 1280 * (kind + 1)] = total[144 * kind : 144 * kind + 128]
        pack_tail(jnp.concatenate([total[128:144], total[272:288]], 1), 8, back)
        for k in (15, 14, 13, 12, 11, 10, 9, 8) if b else (7, 6, 5, 4, 3, 2, 1):
            give_back(k).start()
    rback[:ROWS] = rsend[:ROWS]

    for i in range(1, 8):
        for kind in range(2):
            regroup(i, kind).wait_send()
    for k in range(1, 16):
        token(k).wait_send()
    for n in range(CHUNKS):
        cross(n).wait_send()
        for step in (1, -1):
            send_x(n, step).wait_send()
            send_on(n, step).wait_send()
        for i in range(4):
            over_core(n, i, c).wait_send()

    def combine(total, b, kind, width):
        lanes = slice(1280 * kind, 1280 * (kind + 1))
        for i in range(2):
            for rows, held in (
                (slice(128 * b, 128 * (b + 1)), rback[128 * b : 128 * (b + 1), lanes]),
                (slice(256 + 16 * b, 256 + 16 * (b + 1)), tails[:, lanes]),
            ):
                total += lax.dot_general(
                    wsel[i, rows, :width], held, (((0,), (0,)), ((), ())), preferred_element_type=F32
                )
        return total

    from_p, from_t = jnp.zeros((256, 1280), F32), jnp.zeros((128, 1280), F32)
    for b in (1, 0):
        for k in range(8 * b, 8 * b + 8):
            if k:
                give_back(k).wait_recv()
        unpack_tail(rback.at[128 * b : 128 * (b + 1)], 8, tails)
        from_p = combine(from_p, b, 0, 256)
        from_t = combine(from_t, b, 1, 128)
    out[:128] = from_p[:128].astype(BF)
    out[128:] = (from_t + from_p[128:]).astype(BF)

    for k in range(1, 16):
        give_back(k).wait_send()


def split(both, out_p, out_t):
    out_p[...] = both[:128]
    out_t[...] = both[128:]


def per_device(*args):
    args = [a.T for a in args[:5]] + list(args[5:])
    vmem, hbm = pl.BlockSpec(memory_space=pltpu.VMEM), pl.BlockSpec(memory_space=pl.ANY)
    dma = pltpu.SemaphoreType.DMA
    both = pl.pallas_call(
        layer,
        out_shape=jax.ShapeDtypeStruct((256, 1280), BF),
        in_specs=[hbm] * 2 + [vmem] * 3 + [hbm] * 3,
        out_specs=vmem,
        scratch_shapes=[
            pltpu.VMEM((2, 1280, 128), BF),
            pltpu.VMEM((256, LANES), BF),
            pltpu.VMEM((256, LANES), BF),
            pltpu.VMEM((256, LANES), BF),
            pltpu.VMEM((256, LANES), BF),
            pltpu.VMEM((4, 1280, 768), BF),
            pltpu.VMEM((1536, 1280), BF),
            pltpu.VMEM((4, 1280, 768), BF),
            pltpu.VMEM((1536, 1280), BF),
            pltpu.VMEM((2, 288, 1280), BF),
            pltpu.VMEM((2, 288, 1536), BF),
            pltpu.VMEM((2, 288, 1280), BF),
            pltpu.VMEM((16, 2560), BF),
            pltpu.VMEM((2, 288, 256), BF),
            dma((9,)),
            dma((2, 16)),
            dma((2, 16)),
            dma((2, 16)),
            dma((2, CHUNKS)),
            dma((2, 2 * CHUNKS)),
            dma((2, 2 * CHUNKS)),
            dma((2, 4 * CHUNKS)),
            pltpu.SemaphoreType.REGULAR,
        ],
        compiler_params=pltpu.CompilerParams(
            collective_id=0, has_side_effects=True, vmem_limit_bytes=60 << 20
        ),
    )(*args)
    return pl.pallas_call(split, out_shape=(jax.ShapeDtypeStruct((128, 1280), BF),) * 2)(both)


def solution(mesh):
    tokens = P(("exp", "seq"), None)
    halves = P("exp", None, None)
    return jax.shard_map(
        per_device,
        mesh=mesh,
        in_specs=(P("exp", "seq"), P("exp", "seq"), tokens, tokens, tokens, halves, halves, halves),
        out_specs=(tokens, tokens),
        check_vma=False,
    )
```

```python
import functools

import jax
import jax.numpy as jnp
from jax import lax
from jax.experimental import pallas as pl
from jax.experimental.pallas import tpu as pltpu
from jax.sharding import PartitionSpec as P

MESH = pl.DeviceIdType.MESH
BF, F32 = jnp.bfloat16, jnp.float32
HOPS = (0, -1, 2, -3)
LANES = 2944
ROWS = 16
CHUNKS = 6


def iota(shape, dim):
    return lax.broadcasted_iota(jnp.int32, shape, dim)


def pack_matrix(n, transposed):
    shape = (ROWS * n, ROWS * n)
    a, b = (iota(shape, 1), iota(shape, 0)) if transposed else (iota(shape, 0), iota(shape, 1))
    k, rho = a >> 4, a & 15
    return (b == (rho >> 1) * (2 * n) + k * 2 + (rho & 1)).astype(BF)


def pack_tail(tail, n, out):
    matrix = pack_matrix(n, False)
    for t in range(3):
        groups = 8 if t < 2 else 4
        stacked = jnp.concatenate([tail[:, 128 * (8 * t + j) : 128 * (8 * t + j + 1)] for j in range(groups)], 0)
        out[:, 2560 + 128 * t : 2560 + 128 * (t + 1)] = jnp.dot(
            matrix[:, : groups * 2 * n], stacked, preferred_element_type=F32
        ).astype(BF)


def unpack_tail(messages, n, out):
    matrix = pack_matrix(n, True)
    for t in range(3):
        groups = 8 if t < 2 else 4
        rows = jnp.dot(
            matrix[: groups * 2 * n], messages[:, 2560 + 128 * t : 2560 + 128 * (t + 1)], preferred_element_type=F32
        ).astype(BF)
        for j in range(groups):
            out[:, 128 * (8 * t + j) : 128 * (8 * t + j + 1)] = rows[2 * n * j : 2 * n * (j + 1)]


def layer(
    hp, ht, ids, gates, slopes, w_gate, w_up, w_down, out,
    toks, sbuf, rcv, rsend, rback, gu_own, dn_own, gu_oth, dn_oth, xin, hid, part, tails, wsel,
    own_sem, rg_sem, tk_sem, rt_sem, z_sem, x_sem, r_sem, c_sem, plane_sem,
):
    seq, ex = lax.axis_index("seq"), lax.axis_index("exp")
    x, c, y, z = seq // 2, lax.rem(seq, 2), ex // 8, lax.rem(ex, 8)
    sgn = 1 - 2 * lax.rem(z, 2)

    ys = [lax.rem(y + j, 4) * 8 for j in range(4)]
    around = [lax.rem(z + 8 + hop * sgn, 8) for hop in (0, 1, 2, -1, -2, -3)]
    xs = [lax.rem(x + i, 4) for i in range(4)]

    def dest(k):
        return (seq, ys[k % 4] + around[(0, 3, 2, 5)[k // 4]])

    def source(k):
        return (seq, ys[-k % 4] + around[(0, 3, 4, 5)[k // 4]])

    partner = (seq, ys[0] + around[1])
    other_core = (2 * x + 1 - c, ex)

    def remote(src, dst, send, recv, device):
        return pltpu.make_async_remote_copy(src, dst, send, recv, device_id=device, device_id_type=MESH)

    barrier = pltpu.get_barrier_semaphore()
    for i in range(1, 8):
        pl.semaphore_signal(barrier, inc=1, device_id=(lax.rem(seq + i, 8), ex), device_id_type=MESH)
    for i in range(1, 8):
        pl.semaphore_signal(barrier, inc=1, device_id=(seq, ys[0] + lax.rem(z + i, 8)), device_id_type=MESH)
    for j in range(1, 4):
        pl.semaphore_signal(barrier, inc=1, device_id=(seq, ys[j] + z), device_id_type=MESH)

    own = [
        pltpu.make_async_copy(w.at[0, :, pl.ds(384 * q, 384)], gu_own.at[q, :, pl.ds(384 * g, 384)], own_sem.at[2 * q + g])
        for q in range(4)
        for g, w in enumerate((w_gate, w_up))
    ]
    own.append(pltpu.make_async_copy(w_down.at[0], dn_own, own_sem.at[8]))
    pl.semaphore_wait(barrier, 17)

    def regroup(i, kind):
        to = lax.rem(seq + i, 8)
        n = 2 * i + kind
        src = (hp, ht)[kind].at[:, pl.ds(pl.multiple_of(to * 128, 128), 128)]
        dst = toks.at[kind, pl.ds(pl.multiple_of(seq * 160, 32), 160)]
        if i == 0:
            return pltpu.make_async_copy(src, dst, rg_sem.at[1, n])
        return remote(src, dst, rg_sem.at[0, n], rg_sem.at[1, n], (to, ex))

    for kind in range(2):
        for i in range(8):
            regroup(i, kind).start()

    def region(n, q, core, half=None, source=False):
        g, sub = n // 2, n % 2
        size = 320 if g < 2 else 96
        first = core * (2 * size) + sub * size
        if half is not None:
            size //= 2
            first += half * size
        if g == 2:
            rows = pl.ds(pl.multiple_of(q * 384 + first, 16), size)
            return w_down.at[0, rows] if source else dn_oth.at[rows]
        rows = pl.ds(pl.multiple_of(first, 16), size)
        if source:
            return (w_gate, w_up)[g].at[0, rows, pl.ds(pl.multiple_of(q * 384, 128), 384)]
        return gu_oth.at[q, rows, pl.ds(384 * g, 384)]

    def cross(n):
        return remote(region(n, x, c, source=True), region(n, x, c), z_sem.at[0, n], z_sem.at[1, n], partner)

    def along(ref, sems, n, step):
        i = 2 * n + (step < 0)
        return remote(ref, ref, sems.at[0, i], sems.at[1, i], (2 * xs[step % 4] + c, ex))

    def send_x(n, step):
        return along(region(n, x, c), x_sem, n, step)

    def recv_x(n, step):
        return along(region(n, xs[-step % 4], c), x_sem, n, step)

    def send_on(n, step):
        return along(region(n, xs[-step % 4], c, half=int(step < 0)), r_sem, n, step)

    def recv_on(n, step):
        return along(region(n, xs[2], c, half=int(step < 0)), r_sem, n, step)

    def over_core(n, i, core):
        ref = region(n, xs[(0, 3, 1, 2)[i]], core)
        return remote(ref, ref, c_sem.at[0, 4 * n + i], c_sem.at[1, 4 * n + i], other_core)

    for n in range(CHUNKS):
        cross(n).start()
    for j in range(1, 4):
        pl.semaphore_signal(plane_sem, inc=1, device_id=(seq, ys[j] + z), device_id_type=MESH)
    for copy in own:
        copy.start()

    def row(ref, k):
        return jnp.broadcast_to(ref[k : k + 1, :].astype(F32), (16, 128))

    k16 = iota((16, 128), 0)
    cls = k16 >> 2
    zk = lax.rem(z + sgn * jnp.where(cls == 0, 0, jnp.where(cls == 1, -1, jnp.where(cls == 2, 2, -3))) + 16, 8)
    named = (4 * lax.rem(y + (k16 & 3), 4) + (zk >> 1)).astype(F32)
    first, second = (row(ids, k) == named for k in range(2))
    member = jnp.logical_or(first, second)
    before = (iota((128, 128), 0) < iota((128, 128), 1)).astype(BF)
    rank = jnp.dot(member.astype(BF), before, preferred_element_type=F32)
    values = [jnp.where(member, rank, -1.0).astype(BF)]
    for ref in (gates, slopes):
        weight = jnp.where(first, row(ref, 0), jnp.where(second, row(ref, 1), 0.0))
        high = weight.astype(BF)
        values += [high, (weight - high.astype(F32)).astype(BF)]
    slot_row = iota((288, 16), 0)
    spread = (jnp.where(slot_row < 256, slot_row >> 4, (slot_row - 256) >> 1) == iota((288, 16), 1)).astype(BF)
    spread = jnp.dot(spread, jnp.concatenate(values, 1), preferred_element_type=F32)
    a = iota((288, 128), 0)
    chosen = spread[:, :128] == jnp.where(a < 256, a & 15, 16 + (a & 1)).astype(F32)
    for i, part_of in enumerate((1, 3, 2, 4)):
        wsel[i // 2, :, 128 * (i % 2) : 128 * (i % 2 + 1)] = jnp.where(
            chosen, spread[:, 128 * part_of : 128 * (part_of + 1)], 0.0
        ).astype(BF)
    chosen = chosen.astype(BF)

    def arrive(n):
        cross(n).wait_recv()
        for step in (1, -1):
            send_x(n, step).start()
        over_core(n, 0, c).start()

    def pass_on(n):
        for i, step in ((1, 1), (2, -1)):
            recv_x(n, step).wait_recv()
            send_on(n, step).start()
            over_core(n, i, c).start()

    def finish(n):
        for step in (1, -1):
            recv_on(n, step).wait_recv()
        over_core(n, 3, c).start()

    def regrouped():
        for kind in range(2):
            regroup(0, kind).wait()
            for i in range(1, 8):
                regroup(i, kind).wait_recv()

    def dispatch(rows, kind):
        return lax.dot_general(
            rows, toks[kind], (((1,), (1,)), ((), ())), preferred_element_type=F32
        ).astype(BF)

    def rows_of(k):
        return pl.ds(ROWS * k, ROWS)

    def token(k):
        return remote(sbuf.at[rows_of(k)], rcv.at[rows_of(k)], tk_sem.at[0, k], tk_sem.at[1, k], dest(k))

    def give_back(k):
        return remote(rsend.at[rows_of(k)], rback.at[rows_of(k)], rt_sem.at[0, k], rt_sem.at[1, k], source(k))

    def send_rows():
        for kind in range(2):
            sbuf[:, 1280 * kind : 1280 * (kind + 1)] = dispatch(chosen[:256], kind)
        pack_tail(jnp.concatenate([dispatch(chosen[256:], kind) for kind in range(2)], 1), 16, sbuf)
        pl.semaphore_wait(plane_sem, 3)
        for first in (0, 2):
            for j in range(4):
                for d in (first + 1, first):
                    if d or j:
                        token(4 * d + j).start()
        rcv[:ROWS] = sbuf[:ROWS]

    def hidden(b, weights):
        @pl.loop(0, 4, unroll=2)
        def _(q):
            both = jnp.dot(xin[b], weights[q], preferred_element_type=F32)
            pre_gate, tan_gate = both[:144, :384], both[144:, :384]
            pre_up, tan_up = both[:144, 384:], both[144:, 384:]
            sigma = jax.nn.sigmoid(pre_gate)
            swish = pre_gate * sigma
            slope = sigma * (1.0 + pre_gate * (1.0 - sigma))
            lanes = pl.ds(pl.multiple_of(q * 384, 128), 384)
            hid[b, :144, lanes] = (swish * pre_up).astype(BF)
            hid[b, 144:, lanes] = (slope * tan_gate * pre_up + swish * tan_up).astype(BF)

    def rows_in(b):
        for k in range(8 * b, 8 * b + 8):
            if k:
                token(k).wait_recv()
        here = rcv.at[128 * b : 128 * (b + 1)]
        unpack_tail(here, 8, tails)
        for kind in range(2):
            xin[b, 144 * kind : 144 * kind + 128] = here[:, 1280 * kind : 1280 * (kind + 1)]
            xin[b, 144 * kind + 128 : 144 * (kind + 1)] = tails[:, 1280 * kind : 1280 * (kind + 1)]

    def own_hidden(b):
        hidden(b, gu_own)

    def own_down(b):
        part[b] = jnp.dot(hid[b], dn_own[...], preferred_element_type=F32).astype(BF)

    def other_hidden(b):
        hidden(b, gu_oth)

    def own_here():
        for copy in own:
            copy.wait()

    def from_core(n):
        for i in range(4):
            over_core(n, i, 1 - c).wait_recv()

    order = (
        (arrive, 0), (regrouped,), (send_rows,), (arrive, 1), (pass_on, 0), (arrive, 2),
        (pass_on, 1), (finish, 0), (arrive, 3), (pass_on, 2), (finish, 1), (own_here,),
        (rows_in, 0), (own_hidden, 0), (arrive, 4), (pass_on, 3), (finish, 2), (own_down, 0),
        (arrive, 5), (pass_on, 4), (finish, 3), (from_core, 0), (from_core, 1), (from_core, 2),
        (from_core, 3), (other_hidden, 0), (rows_in, 1), (pass_on, 5), (own_hidden, 1), (finish, 4),
        (own_down, 1), (other_hidden, 1), (finish, 5), (from_core, 4), (from_core, 5),
    )
    for step, *arg in order:
        step(*arg)
    for b in (1, 0):
        here = jnp.dot(hid[b], dn_oth[...], preferred_element_type=F32).astype(BF)
        total = (here.astype(F32) + part[b].astype(F32)).astype(BF)
        back = rsend.at[128 * b : 128 * (b + 1)]
        for kind in range(2):
            back[:, 1280 * kind : 1280 * (kind + 1)] = total[144 * kind : 144 * kind + 128]
        pack_tail(jnp.concatenate([total[128:144], total[272:288]], 1), 8, back)
        for k in (15, 14, 13, 12, 11, 10, 9, 8) if b else (7, 6, 5, 4, 3, 2, 1):
            give_back(k).start()
    rback[:ROWS] = rsend[:ROWS]

    for i in range(1, 8):
        for kind in range(2):
            regroup(i, kind).wait_send()
    for k in range(1, 16):
        token(k).wait_send()
    for n in range(CHUNKS):
        cross(n).wait_send()
        for step in (1, -1):
            send_x(n, step).wait_send()
            send_on(n, step).wait_send()
        for i in range(4):
            over_core(n, i, c).wait_send()

    def combine(total, b, kind, width):
        lanes = slice(1280 * kind, 1280 * (kind + 1))
        for i in range(2):
            for rows, held in (
                (slice(128 * b, 128 * (b + 1)), rback[128 * b : 128 * (b + 1), lanes]),
                (slice(256 + 16 * b, 256 + 16 * (b + 1)), tails[:, lanes]),
            ):
                total += lax.dot_general(
                    wsel[i, rows, :width], held, (((0,), (0,)), ((), ())), preferred_element_type=F32
                )
        return total

    from_p, from_t = jnp.zeros((256, 1280), F32), jnp.zeros((128, 1280), F32)
    for b in (1, 0):
        for k in range(8 * b, 8 * b + 8):
            if k:
                give_back(k).wait_recv()
        unpack_tail(rback.at[128 * b : 128 * (b + 1)], 8, tails)
        from_p = combine(from_p, b, 0, 256)
        from_t = combine(from_t, b, 1, 128)
    out[:128] = from_p[:128].astype(BF)
    out[128:] = (from_t + from_p[128:]).astype(BF)

    for k in range(1, 16):
        give_back(k).wait_send()


def split(both, out_p, out_t):
    out_p[...] = both[:128]
    out_t[...] = both[128:]


def per_device(*args):
    args = [a.T for a in args[:5]] + list(args[5:])
    vmem, hbm = pl.BlockSpec(memory_space=pltpu.VMEM), pl.BlockSpec(memory_space=pl.ANY)
    dma = pltpu.SemaphoreType.DMA
    both = pl.pallas_call(
        layer,
        out_shape=jax.ShapeDtypeStruct((256, 1280), BF),
        in_specs=[hbm] * 2 + [vmem] * 3 + [hbm] * 3,
        out_specs=vmem,
        scratch_shapes=[
            pltpu.VMEM((2, 1280, 128), BF),
            pltpu.VMEM((256, LANES), BF),
            pltpu.VMEM((256, LANES), BF),
            pltpu.VMEM((256, LANES), BF),
            pltpu.VMEM((256, LANES), BF),
            pltpu.VMEM((4, 1280, 768), BF),
            pltpu.VMEM((1536, 1280), BF),
            pltpu.VMEM((4, 1280, 768), BF),
            pltpu.VMEM((1536, 1280), BF),
            pltpu.VMEM((2, 288, 1280), BF),
            pltpu.VMEM((2, 288, 1536), BF),
            pltpu.VMEM((2, 288, 1280), BF),
            pltpu.VMEM((16, 2560), BF),
            pltpu.VMEM((2, 288, 256), BF),
            dma((9,)),
            dma((2, 16)),
            dma((2, 16)),
            dma((2, 16)),
            dma((2, CHUNKS)),
            dma((2, 2 * CHUNKS)),
            dma((2, 2 * CHUNKS)),
            dma((2, 4 * CHUNKS)),
            pltpu.SemaphoreType.REGULAR,
        ],
        compiler_params=pltpu.CompilerParams(
            collective_id=0, has_side_effects=True, vmem_limit_bytes=60 << 20
        ),
    )(*args)
    return pl.pallas_call(split, out_shape=(jax.ShapeDtypeStruct((128, 1280), BF),) * 2)(both)


def solution(mesh):
    tokens = P(("exp", "seq"), None)
    halves = P("exp", None, None)
    return jax.shard_map(
        per_device,
        mesh=mesh,
        in_specs=(P("exp", "seq"), P("exp", "seq"), tokens, tokens, tokens, halves, halves, halves),
        out_specs=(tokens, tokens),
        check_vma=False,
    )
```
